32 devices in a mesh: clu: 8 (over z, y), sub: 4 (over x, core).
Axes of the slice: x: 2, y: 2, z: 4, core: 2. Of those that a mesh axis runs over, the one named last changes fastest.
Arguments:
- operator: bfloat16 [32, 1024, 1024], P(('clu', 'sub')), as said below
- rhs: float32 [32, 1024, 128], P(('clu', 'sub')), may hold values from -6 to 6
- interface_sizes: int32 [32], P(('clu', 'sub')), may hold values from 64 to 1024, as said below
- neighbour_rows: int32 [32, 1024], P(('clu', 'sub')), may hold values from 0 to 1023, each once within a row
- kept_columns: int32 [1, 128], replicated, may hold values 0 or 1
Outputs:
- solution: float32 [32, 1024, 128], P(('clu', 'sub'))
- residual: float32 [32, 1024, 128], P(('clu', 'sub'))
- direction: float32 [32, 1024, 128], P(('clu', 'sub'))
The draws below stay inside these ranges and needn't reach their ends.
Inputs may be any that keep to these rules, and one draw needn't show every extreme that they name: `operator`: each subdomain's block is symmetric positive definite. `interface_sizes`: some subdomain has all 1024 multipliers live in every draw. `neighbour_rows`: each row is a permutation of 0 to 1023.
All inputs are finite; a program needn't handle non-finite values.
Results may differ from the reference program's by a relative error of at most 0.0065.
Values may be sent and summed in bfloat16 or wider, within the bound.
No kernel may reach another device: no remote copies, remote signals or barrier semaphores. Data moves between devices by JAX's collectives and lax.ppermute only.
A program may use at most 64 MiB of HBM per device.

```python
import math
import jax
import jax.numpy as jnp
from jax import lax

MULT = 1024
DIRS = 128
ITERS = 1
SUBS = 32
N_CLU = 8
N_SUB = 4


def draw_operator(key, part):

    def single(subdomain):
        folded = jax.random.fold_in(key, subdomain)
        subkeys = jax.random.split(folded, 2)
        entries = jax.random.normal(subkeys[0], (MULT, MULT), jnp.float32)
        symmetric = (entries + entries.T) * (0.5 * MULT ** (-0.5))
        diagonal = 2.0 * jnp.exp(jax.random.uniform(subkeys[1], (MULT,), jnp.float32) * math.log(3.0))
        return (symmetric + jnp.diag(diagonal)).astype(jnp.bfloat16)
    return lax.map(single, jnp.arange(SUBS))


def draw_interface_sizes(key, part):
    first, second, third = jax.random.split(jax.random.fold_in(key, 17), 3)
    base = jax.random.randint(first, (SUBS,), MULT // 16, MULT // 8 + 1)
    power = jax.random.randint(second, (SUBS,), 0, 4)
    sizes = jnp.minimum(MULT, jnp.left_shift(base, power))
    chosen = jax.random.randint(third, (), 0, SUBS)
    return jnp.where(jnp.arange(SUBS) == chosen, MULT, sizes).astype(jnp.int32)


def touch_ends(values, rng, least, high):
    extent = values.shape
    place = [jax.random.randint(jax.random.fold_in(rng, axis), (), 0, extent[axis]) for axis in range(len(extent))]
    values = values.at[tuple(place)].set(least)
    longest = extent.index(max(extent))
    place[longest] = (place[longest] + 1) % extent[longest]
    return values.at[tuple(place)].set(high)


def steps_of(own_key, shape, cuts, low, high):
    gain = 1.0
    for dim, blocks in cuts:
        heights = jax.random.uniform(jax.random.fold_in(jax.random.fold_in(own_key, 6), dim), (blocks,), jnp.float32, low / len(cuts), high / len(cuts))
        gain = gain * jnp.repeat(jnp.exp(heights), shape[dim] // blocks).reshape((-1,) + (1,) * (len(shape) - 1 - dim))
    return gain


def scatter_about(stream_key, extent, spread, bound, shards=(), dtype=jnp.bfloat16):
    level = steps_of(stream_key, extent, shards, -0.22, 0.18) if shards else 1.0
    array = jax.random.normal(stream_key, extent, jnp.float32) * spread * level
    return jnp.minimum(jnp.maximum(array, -bound), bound).astype(dtype)


def setup_inputs(seed: int = 0) -> dict:
    splits = jax.random.split(jax.random.key(seed), 6)
    return {
        "operator": draw_operator(jax.random.fold_in(splits[5], 71), 0),
        "rhs": scatter_about(splits[1], (SUBS, MULT, DIRS), 1.0, 6.0, ((0, 32),), jnp.float32),
        "interface_sizes": draw_interface_sizes(jax.random.fold_in(splits[5], 71), 0),
        "neighbour_rows": jax.vmap(lambda own: jax.random.permutation(own, MULT))(jax.random.split(splits[3], SUBS)).reshape((SUBS, MULT)).astype(jnp.int32),
        "kept_columns": touch_ends((jax.random.randint(splits[4], (ITERS, DIRS), 0, 4) < 3).astype(jnp.int32), jax.random.fold_in(splits[4], 1), 0, 1),
    }


stiffness = 1.0

def apply_operator(operator, rounded, neighbour_rows, inverse, degree, rowmask):
    product = lax.map(lambda operands: jnp.dot(operands[0].astype(jnp.float32), operands[1].astype(jnp.float32), preferred_element_type=jnp.float32), (operator, rounded))
    grid = rounded.reshape(N_CLU, N_SUB, MULT, DIRS)
    ahead = jnp.take_along_axis(rounded, inverse[:, :, None], axis=1).reshape(N_CLU, N_SUB, MULT, DIRS)
    empty = jnp.zeros_like(grid[:1])
    behind = jnp.concatenate([empty, grid[:-1]], 0).reshape(SUBS, MULT, DIRS)
    left_rows = jnp.take_along_axis(behind, neighbour_rows[:, :, None], axis=1)
    right_rows = jnp.concatenate([ahead[1:], empty], 0).reshape(SUBS, MULT, DIRS)
    coupling = degree * rounded.astype(jnp.float32) - left_rows.astype(jnp.float32) - right_rows.astype(jnp.float32)
    return rowmask * (product + stiffness * coupling)

def reference(operator, rhs, interface_sizes, neighbour_rows, kept_columns):
    highest = lax.Precision.HIGHEST
    rowmask = (jnp.arange(MULT)[None, :] < interface_sizes[:, None]).astype(jnp.float32)[:, :, None]
    inverse = jnp.argsort(neighbour_rows, axis=1)
    position = jnp.arange(SUBS) // N_SUB
    degree = ((position > 0).astype(jnp.float32) + (position < N_CLU - 1).astype(jnp.float32))[:, None, None]
    residual = rhs * rowmask
    solution = jnp.zeros_like(residual)
    direction = residual
    for iteration in range(ITERS):
        keep = kept_columns[iteration].astype(jnp.float32)
        rounded = (direction * keep[None, None, :]).astype(jnp.bfloat16)
        image = apply_operator(operator, rounded, neighbour_rows, inverse, degree, rowmask)
        widened = rounded.astype(jnp.float32)
        curvature = jnp.einsum('smk,sml->kl', widened, image, precision=highest)
        projected = jnp.einsum('smk,sml->kl', widened, residual, precision=highest)
        regular = curvature + jnp.diag(1.0 - keep)
        factor = jnp.linalg.cholesky(regular)
        weights = jax.scipy.linalg.cho_solve((factor, True), projected)
        solution = solution + jnp.einsum('smk,kl->sml', widened, weights, precision=highest)
        residual = residual - jnp.einsum('smk,kl->sml', image, weights, precision=highest)
        coupled = jnp.einsum('smk,sml->kl', image, residual, precision=highest)
        correction = jax.scipy.linalg.cho_solve((factor, True), coupled)
        direction = residual - jnp.einsum('smk,kl->sml', widened, correction, precision=highest)
    return (solution, residual, direction)
```

```python
import functools
import itertools

import jax
import jax.numpy as jnp
from jax import lax
from jax.experimental import pallas as pl
from jax.experimental.pallas import tpu as pltpu
from jax.sharding import PartitionSpec as P

stiffness = 1.0
f32 = jnp.float32
bf16 = jnp.bfloat16
AXES = ("clu", "sub")
VMEM_BYTES = 24 * 2**20
SMEM = pl.BlockSpec(memory_space=pltpu.SMEM)
SIZE, PLACE, LAST, CORE = range(4)


def dot(a, b):
    return jnp.dot(a, b, preferred_element_type=f32)


def exact(a, b):
    return jnp.dot(a, b, preferred_element_type=f32, precision=lax.Precision.HIGHEST)


def gram(a, b):
    return lax.dot_general(a, b, (((0,), (0,)), ((), ())), preferred_element_type=f32)


def two_parts(values):
    upper = values.astype(bf16)
    return upper, (values - upper.astype(f32)).astype(bf16)


def parameters():
    return pltpu.CompilerParams(vmem_limit_bytes=VMEM_BYTES)


def live_rows(scalars, start, rows, columns):
    return start + lax.broadcasted_iota(jnp.int32, (rows, columns), 0) < scalars[SIZE]


def round_kernel(scalars, rhs, kept, pairing, out):
    height, breadth = rhs.shape
    keep = kept[...].astype(f32)
    block = jnp.where(live_rows(scalars, 0, height, breadth), rhs[...], 0.0) * keep
    out[0:height, :] = block.astype(bf16)
    rows = pairing[...]
    digits = jnp.concatenate([rows // 256, rows % 256], 0)
    out[height:, :] = digits.astype(f32).astype(bf16)


def local_kernel(scalars, operator, packed, out):
    height = out.shape[0]
    place = scalars[PLACE]
    degree = (place > 0).astype(f32) + (place < scalars[LAST]).astype(f32)
    step = min(height, 256)
    for start in range(0, height, step):
        rows = slice(start, start + step)
        out[rows, :] = dot(operator[rows, :], packed[0:height, :]) + (
            stiffness * degree
        ) * packed[rows, :].astype(f32)


def picked(block, pairing, start, rows, inverse):
    count, lanes = pairing.shape
    strips = []
    if inverse:
        place = (start + lax.broadcasted_iota(jnp.int32, (rows, lanes), 0)).astype(f32)
        for k in range(count):
            strips.append(jnp.where(place == pairing[k : k + 1, :], 1.0, 0.0).astype(bf16))
        chosen = jnp.concatenate(strips, 1)
    else:
        column = lax.broadcasted_iota(jnp.int32, (lanes, lanes), 1).astype(f32)
        for first in range(start, start + rows, lanes):
            k = first // lanes
            wanted = jnp.broadcast_to(pairing[k : k + 1, :], (lanes, lanes)).T
            strips.append(
                jnp.concatenate(
                    [
                        jnp.where(wanted == column + float(j * lanes), 1.0, 0.0).astype(bf16)
                        for j in range(count)
                    ],
                    1,
                )
            )
        chosen = jnp.concatenate(strips, 0)
    return dot(chosen, block)


def sent_pairing(packed, height):
    digits = packed[height:, :].astype(f32)
    half = digits.shape[0] // 2
    return digits[:half] * 256.0 + digits[half:]


def near_kernel(scalars, pairing, other, base, out):
    height = base.shape[0]
    step = min(height, 256)
    even = scalars[PLACE] % 2 == 0

    def go(rows_of, inverse):
        for start in range(0, height, step):
            rows = slice(start, start + step)
            out[rows, :] = base[rows, :] - stiffness * picked(
                other[0:height, :], rows_of, start, step, inverse
            )

    @pl.when(even)
    def _():
        go(sent_pairing(other, height), True)

    @pl.when(jnp.logical_not(even))
    def _():
        go(pairing[...].astype(f32), False)


def sums_kernel(scalars, pairing, other, base, packed, rhs, upper, lower, mine, theirs, image, stack):
    height, breadth = base.shape
    step = min(height, 256)
    even = scalars[PLACE] % 2 == 0

    def go(rows_of, inverse):
        for start in range(0, height, step):
            rows = slice(start, start + step)
            whole = base[rows, :] - stiffness * picked(
                other[0:height, :], rows_of, start, step, inverse
            )
            image[rows, :] = jnp.where(live_rows(scalars, start, step, breadth), whole, 0.0)

    @pl.when(even)
    def _():
        go(pairing[...].astype(f32), False)

    @pl.when(jnp.logical_not(even))
    def _():
        go(sent_pairing(other, height), True)

    high, low = two_parts(image[...])
    upper[...] = high
    lower[...] = low
    residual = jnp.where(live_rows(scalars, 0, height, breadth), rhs[...], 0.0)
    res_high, res_low = two_parts(residual)
    right = jnp.concatenate([high, low, res_high, res_low], 1)
    first = gram(packed[0:height, :], right)
    second = gram(high, right)
    third = gram(low, res_high)
    b = breadth
    curvature = first[:, 0:b] + first[:, b : 2 * b]
    projected = first[:, 2 * b : 3 * b] + first[:, 3 * b :]
    mixed = second[:, b : 2 * b]
    squares = second[:, 0:b] + mixed + mixed.T
    cross = second[:, 2 * b : 3 * b] + second[:, 3 * b :] + third
    row = lax.broadcasted_iota(jnp.int32, (b, b), 0)
    column = lax.broadcasted_iota(jnp.int32, (b, b), 1)
    diagonal = jnp.sum(jnp.where(row == column, squares, 0.0), axis=0, keepdims=True)
    stack[0:b, :] = jnp.where(row >= column, curvature, squares)
    stack[b : 2 * b, :] = projected
    stack[2 * b : 3 * b, :] = cross
    stack[3 * b :, :] = jnp.broadcast_to(diagonal, (stack.shape[0] - 3 * b, b))
    half = mine.shape[0]
    core = scalars[CORE]
    mine[...] = stack[pl.ds(pl.multiple_of(core * half, 8), half), :]
    theirs[...] = stack[pl.ds(pl.multiple_of((1 - core) * half, 8), half), :]


def inverse_of(regular, eye, total, power):
    size = regular.shape[0]
    one = eye.astype(f32)
    kept = jnp.where(eye, regular, 0.0)
    scale_row = lax.rsqrt(jnp.sum(kept, axis=0, keepdims=True))
    scale_column = lax.rsqrt(jnp.sum(kept, axis=1, keepdims=True))
    scaled = regular * scale_row * scale_column
    error = one - scaled
    square = exact(error, error)
    size_of_square = jnp.sum(square * square)
    total[...] = one + error
    power[...] = square

    @pl.when(size_of_square >= 0.5)
    def _():
        c = 1.0 / jnp.max(jnp.sum(jnp.abs(scaled), axis=0, keepdims=True))
        smaller = one - c * scaled
        total[...] = c * (one + smaller)
        power[...] = exact(smaller, smaller)

    def more(state):
        count, norm = state
        return jnp.logical_and(norm > 1e-6, count < 48)

    def again(state):
        count, _ = state
        now = power[...]
        both = exact(jnp.concatenate([total[...], now], 0), now)
        total[...] = total[...] + both[:size]
        power[...] = both[size:]
        return count + 1, jnp.sum(both[size:] * both[size:])

    started = jnp.sum(power[...] * power[...])
    lax.while_loop(more, again, (jnp.int32(0), started))
    guess = total[...]
    better = guess + exact(guess, one - exact(scaled, guess))
    return better * scale_row * scale_column


def finish_kernel(
    scalars, kept, mine, theirs, packed, upper, lower, rhs, solution, residual, direction,
    stack, both, total, power,
):
    rows, b = solution.shape
    start = pl.program_id(0) * rows

    @pl.when(pl.program_id(0) == 0)
    def _():
        half = mine.shape[0]
        core = scalars[CORE]
        stack[pl.ds(pl.multiple_of(core * half, 8), half), :] = mine[...]
        stack[pl.ds(pl.multiple_of((1 - core) * half, 8), half), :] = theirs[...]
        keep = kept[...].astype(f32)
        row = lax.broadcasted_iota(jnp.int32, (b, b), 0)
        column = lax.broadcasted_iota(jnp.int32, (b, b), 1)
        eye = row == column
        shared = stack[0:b, :]
        turned = shared.T
        regular = jnp.where(row >= column, shared, turned)
        regular = regular + jnp.where(eye, jnp.broadcast_to(1.0 - keep, (b, b)), 0.0)
        diagonal = jnp.broadcast_to(stack[3 * b : 3 * b + 1, :], (b, b))
        squares = jnp.where(row < column, shared, jnp.where(eye, diagonal, turned))
        inverse = inverse_of(regular, eye, total, power)
        weights = exact(inverse, stack[b : 2 * b, :])
        coupled = stack[2 * b : 3 * b, :] - exact(squares, weights)
        correction = exact(inverse, coupled)
        both[...] = jnp.concatenate(two_parts(weights) + two_parts(correction), 1)

    block = packed[...]
    products = dot(block, both[...])
    solution[...] = products[:, 0:b] + products[:, b : 2 * b]
    moved = dot(upper[...], both[:, 0 : 2 * b])
    moved = moved[:, 0:b] + moved[:, b:] + dot(lower[...], both[:, 0:b])
    rest = jnp.where(live_rows(scalars, start, rows, b), rhs[...], 0.0) - moved
    residual[...] = rest
    direction[...] = rest - (products[:, 2 * b : 3 * b] + products[:, 3 * b :])


def factors(number):
    found, p = [], 2
    while number > 1:
        while number % p == 0:
            found.append(p)
            number //= p
        p += 1
    return found


def rounds_of(clusters, places):
    digits, stride = [], 2
    for radix in factors(places // 2) + factors(clusters):
        digits.append((stride, radix))
        stride *= radix
    groups = []
    for digit in digits:
        if groups and len(groups[-1]) == 1 and groups[-1][0][1] * digit[1] <= 4:
            groups[-1].append(digit)
        else:
            groups.append([digit])

    def moves(group):
        offsets = itertools.product(*[range(radix) for _, radix in reversed(group)])
        return [list(zip(reversed(group), o)) for o in offsets if any(o)]

    def moved(index, move):
        for (stride, radix), offset in move:
            digit = index // stride % radix
            index += ((digit + offset) % radix - digit) * stride
        return index

    forward = [moves(g) for g in groups]
    backward = forward[::-1]
    if [len(m) for m in forward] != [len(m) for m in backward]:
        backward = forward
    count = clusters * places
    return [
        [
            [(i, moved(i, (first, second)[i % 2])) for i in range(count)]
            for first, second in zip(ours, others)
        ]
        for ours, others in zip(forward, backward)
    ]


def per_device(clusters, places, operator, rhs, interface_sizes, neighbour_rows, kept_columns):
    matrix, right_side = operator[0], rhs[0]
    height, breadth = right_side.shape
    place = lax.axis_index("clu")
    core = lax.axis_index("sub") % 2
    scalars = jnp.stack(
        [interface_sizes[0], place, jnp.int32(clusters - 1), core]
    ).astype(jnp.int32)
    pairing = neighbour_rows.reshape(height // breadth, breadth)
    extra = 2 * pairing.shape[0]
    like = jax.ShapeDtypeStruct
    whole = lambda *shape: pl.BlockSpec(shape, lambda *_: (0,) * len(shape))
    packed = pl.pallas_call(
        round_kernel,
        out_shape=like((height + extra, breadth), bf16),
        in_specs=[SMEM] + [pl.BlockSpec(memory_space=pltpu.VMEM)] * 3,
        compiler_params=parameters(),
        name="round",
    )(scalars, right_side, kept_columns, pairing)
    other = lax.ppermute(packed, "clu", [(i, i ^ 1) for i in range(clusters) if i ^ 1 < clusters])
    base = pl.pallas_call(
        local_kernel,
        out_shape=like((height, breadth), f32),
        in_specs=[SMEM] + [pl.BlockSpec(memory_space=pltpu.VMEM)] * 2,
        compiler_params=parameters(),
        cost_estimate=pl.CostEstimate(
            flops=2 * height * height * breadth, bytes_accessed=2 * height * height, transcendentals=0
        ),
        name="local",
    )(scalars, matrix, packed)
    onward = [(i, i + 2) for i in range(0, clusters - 2, 2)]
    onward += [(i, i - 2) for i in range(3, clusters, 2)]
    outside = lax.ppermute(other, "clu", onward)
    nearer = pl.pallas_call(
        near_kernel,
        out_shape=like((height, breadth), f32),
        in_specs=[SMEM] + [pl.BlockSpec(memory_space=pltpu.VMEM)] * 3,
        compiler_params=parameters(),
        cost_estimate=pl.CostEstimate(
            flops=2 * height * height * breadth, bytes_accessed=2 * height * height, transcendentals=0
        ),
        name="near",
    )(scalars, pairing, other, base)
    half = (3 * breadth + 16) // 2
    upper, lower, mine, theirs = pl.pallas_call(
        sums_kernel,
        out_shape=(
            like((height, breadth), bf16),
            like((height, breadth), bf16),
            like((half, breadth), f32),
            like((half, breadth), f32),
        ),
        in_specs=[SMEM] + [pl.BlockSpec(memory_space=pltpu.VMEM)] * 5,
        scratch_shapes=[
            pltpu.VMEM((height, breadth), f32),
            pltpu.VMEM((2 * half, breadth), f32),
        ],
        compiler_params=parameters(),
        name="sums",
    )(scalars, pairing, outside, nearer, packed, right_side)
    swap = [(i, i ^ 1) for i in range(clusters * places)]
    mine = mine + lax.ppermute(theirs, AXES, swap)
    for routes in rounds_of(clusters, places):
        parts = [mine] + [lax.ppermute(mine, AXES, route) for route in routes]
        while len(parts) > 1:
            parts = [sum(parts[i : i + 2][1:], parts[i]) for i in range(0, len(parts), 2)]
        mine = parts[0]
    theirs = lax.ppermute(mine, AXES, swap)
    tile = min(height, 256)
    rows = pl.BlockSpec((tile, breadth), lambda i: (i, 0))
    outs = pl.pallas_call(
        finish_kernel,
        grid=(height // tile,),
        out_shape=(like((height, breadth), f32),) * 3,
        in_specs=[SMEM, whole(1, breadth), whole(half, breadth), whole(half, breadth)] + [rows] * 4,
        out_specs=(rows,) * 3,
        scratch_shapes=[
            pltpu.VMEM((2 * half, breadth), f32),
            pltpu.VMEM((breadth, 4 * breadth), bf16),
            pltpu.VMEM((breadth, breadth), f32),
            pltpu.VMEM((breadth, breadth), f32),
        ],
        compiler_params=parameters(),
        name="finish",
    )(scalars, kept_columns, mine, theirs, packed, upper, lower, right_side)
    return tuple(out[None] for out in outs)


def solution(mesh):
    clusters, places = mesh.shape["clu"], mesh.shape["sub"]
    return jax.shard_map(
        functools.partial(per_device, clusters, places),
        mesh=mesh,
        in_specs=(
            P(("clu", "sub"), None, None),
            P(("clu", "sub"), None, None),
            P(("clu", "sub")),
            P(("clu", "sub"), None),
            P(),
        ),
        out_specs=(P(("clu", "sub"), None, None),) * 3,
        check_vma=False,
    )
```

```python
import functools
import itertools

import jax
import jax.numpy as jnp
from jax import lax
from jax.experimental import pallas as pl
from jax.experimental.pallas import tpu as pltpu
from jax.sharding import PartitionSpec as P

stiffness = 1.0
f32 = jnp.float32
bf16 = jnp.bfloat16
AXES = ("clu", "sub")
VMEM_BYTES = 24 * 2**20
COPIES = 4
SMEM = pl.BlockSpec(memory_space=pltpu.SMEM)
VMEM = pl.BlockSpec(memory_space=pltpu.VMEM)
HBM = pl.BlockSpec(memory_space=pltpu.HBM)
SIZE, PLACE, LAST, CORE = range(4)


def dot(a, b):
    return jnp.dot(a, b, preferred_element_type=f32)


def exact(a, b):
    return jnp.dot(a, b, preferred_element_type=f32, precision=lax.Precision.HIGHEST)


def gram(a, b):
    return lax.dot_general(a, b, (((0,), (0,)), ((), ())), preferred_element_type=f32)


def two_parts(values):
    upper = values.astype(bf16)
    return upper, (values - upper.astype(f32)).astype(bf16)


def parameters():
    return pltpu.CompilerParams(vmem_limit_bytes=VMEM_BYTES)


def in_hbm(array):
    return pltpu.with_memory_space_constraint(array, pltpu.HBM)


def live_rows(scalars, start, rows, columns):
    return start + lax.broadcasted_iota(jnp.int32, (rows, columns), 0) < scalars[SIZE]


def round_kernel(sizes, rhs, kept, pairing, out, block, flags, rows, done):
    copies = [
        pltpu.make_async_copy(source, target, done.at[i])
        for i, (source, target) in enumerate(
            [(rhs, block), (kept, flags), (pairing, rows)]
        )
    ]
    for copy in copies:
        copy.start()
    for copy in copies:
        copy.wait()
    height, breadth = block.shape
    live = lax.broadcasted_iota(jnp.int32, (height, breadth), 0) < sizes[0]
    keep = flags[...].astype(f32)
    out[0:height, :] = (jnp.where(live, block[...], 0.0) * keep).astype(bf16)
    order = rows[...]
    digits = jnp.concatenate([order // 256, order % 256], 0)
    out[height:, :] = digits.astype(f32).astype(bf16)


def local_kernel(scalars, operator, packed, out):
    rows, height = operator.shape
    place = scalars[PLACE]
    degree = (place > 0).astype(f32) + (place < scalars[LAST]).astype(f32)
    here = pl.ds(pl.multiple_of(pl.program_id(0) * rows, rows), rows)
    own = packed[here, :].astype(f32)
    out[here, :] = dot(operator[...], packed[0:height, :]) + (stiffness * degree) * own


def picked(block, pairing, start, rows, inverse):
    count, lanes = pairing.shape
    strips = []
    if inverse:
        place = (start + lax.broadcasted_iota(jnp.int32, (rows, lanes), 0)).astype(f32)
        for k in range(count):
            strips.append(jnp.where(place == pairing[k : k + 1, :], 1.0, 0.0).astype(bf16))
        chosen = jnp.concatenate(strips, 1)
    else:
        column = lax.broadcasted_iota(jnp.int32, (lanes, lanes), 1).astype(f32)
        for first in range(start, start + rows, lanes):
            k = first // lanes
            wanted = jnp.broadcast_to(pairing[k : k + 1, :], (lanes, lanes)).T
            strips.append(
                jnp.concatenate(
                    [
                        jnp.where(wanted == column + float(j * lanes), 1.0, 0.0).astype(bf16)
                        for j in range(count)
                    ],
                    1,
                )
            )
        chosen = jnp.concatenate(strips, 0)
    return dot(chosen, block)


def sent_pairing(packed, height):
    digits = packed[height:, :].astype(f32)
    half = digits.shape[0] // 2
    return digits[:half] * 256.0 + digits[half:]


def near_kernel(scalars, pairing, other, base, out):
    height = base.shape[0]
    step = min(height, 256)
    even = scalars[PLACE] % 2 == 0

    def go(rows_of, inverse):
        for start in range(0, height, step):
            rows = slice(start, start + step)
            out[rows, :] = base[rows, :] - stiffness * picked(
                other[0:height, :], rows_of, start, step, inverse
            )

    @pl.when(even)
    def _():
        go(sent_pairing(other, height), True)

    @pl.when(jnp.logical_not(even))
    def _():
        go(pairing[...].astype(f32), False)


def sums_kernel(scalars, pairing, other, base, packed, rhs, upper, lower, mine, theirs, image, stack):
    height, breadth = base.shape
    step = min(height, 256)
    even = scalars[PLACE] % 2 == 0

    def go(rows_of, inverse):
        for start in range(0, height, step):
            rows = slice(start, start + step)
            whole = base[rows, :] - stiffness * picked(
                other[0:height, :], rows_of, start, step, inverse
            )
            image[rows, :] = jnp.where(live_rows(scalars, start, step, breadth), whole, 0.0)

    @pl.when(even)
    def _():
        go(pairing[...].astype(f32), False)

    @pl.when(jnp.logical_not(even))
    def _():
        go(sent_pairing(other, height), True)

    high, low = two_parts(image[...])
    upper[...] = high
    lower[...] = low
    residual = jnp.where(live_rows(scalars, 0, height, breadth), rhs[...], 0.0)
    res_high, res_low = two_parts(residual)
    right = jnp.concatenate([high, low, res_high, res_low], 1)
    first = gram(packed[0:height, :], right)
    second = gram(high, right)
    third = gram(low, res_high)
    b = breadth
    curvature = first[:, 0:b] + first[:, b : 2 * b]
    projected = first[:, 2 * b : 3 * b] + first[:, 3 * b :]
    mixed = second[:, b : 2 * b]
    squares = second[:, 0:b] + mixed + mixed.T
    cross = second[:, 2 * b : 3 * b] + second[:, 3 * b :] + third
    row = lax.broadcasted_iota(jnp.int32, (b, b), 0)
    column = lax.broadcasted_iota(jnp.int32, (b, b), 1)
    diagonal = jnp.sum(jnp.where(row == column, squares, 0.0), axis=0, keepdims=True)
    stack[0:b, :] = jnp.where(row >= column, curvature, squares)
    stack[b : 2 * b, :] = projected
    stack[2 * b : 3 * b, :] = cross
    stack[3 * b :, :] = jnp.broadcast_to(diagonal, (stack.shape[0] - 3 * b, b))
    half = mine.shape[0]
    core = scalars[CORE]
    mine[...] = stack[pl.ds(pl.multiple_of(core * half, 8), half), :]
    theirs[...] = stack[pl.ds(pl.multiple_of((1 - core) * half, 8), half), :]


def inverse_of(regular, eye, total, power):
    size = regular.shape[0]
    one = eye.astype(f32)
    kept = jnp.where(eye, regular, 0.0)
    scale_row = lax.rsqrt(jnp.sum(kept, axis=0, keepdims=True))
    scale_column = lax.rsqrt(jnp.sum(kept, axis=1, keepdims=True))
    scaled = regular * scale_row * scale_column
    error = one - scaled

    def factor(guess, now):
        both = exact(jnp.concatenate([guess, now], 0), now)
        return guess + both[:size], both[size:]

    guess, now = factor(*factor(one + error, exact(error, error)))
    total[...] = guess + exact(guess, now)

    @pl.when(jnp.logical_not(jnp.sum(now * now) < 1e-6))
    def _():
        c = 1.0 / jnp.max(jnp.sum(jnp.abs(scaled), axis=0, keepdims=True))
        smaller = one - c * scaled
        total[...] = c * (one + smaller)
        first = exact(smaller, smaller)
        power[...] = first

        def more(state):
            count, norm = state
            return jnp.logical_and(norm > 1e-6, count < 48)

        def again(state):
            guess, now = factor(total[...], power[...])
            total[...] = guess
            power[...] = now
            return state[0] + 1, jnp.sum(now * now)

        lax.while_loop(more, again, (jnp.int32(0), jnp.sum(first * first)))
        guess = total[...]
        total[...] = guess + exact(guess, one - exact(scaled, guess))

    return total[...] * scale_row * scale_column


def finish_kernel(
    scalars, kept, mine, theirs, packed, upper, lower, rhs, solution, residual, direction,
    stack, total, power, results, done,
):
    height, b = rhs.shape
    rows = results.shape[1] // COPIES
    half = mine.shape[0]
    core = scalars[CORE]
    stack[pl.ds(pl.multiple_of(core * half, 8), half), :] = mine[...]
    stack[pl.ds(pl.multiple_of((1 - core) * half, 8), half), :] = theirs[...]
    keep = kept[...].astype(f32)
    row = lax.broadcasted_iota(jnp.int32, (b, b), 0)
    column = lax.broadcasted_iota(jnp.int32, (b, b), 1)
    eye = row == column
    shared = stack[0:b, :]
    turned = shared.T
    regular = jnp.where(row >= column, shared, turned)
    regular = regular + jnp.where(eye, jnp.broadcast_to(1.0 - keep, (b, b)), 0.0)
    diagonal = jnp.broadcast_to(stack[3 * b : 3 * b + 1, :], (b, b))
    squares = jnp.where(row < column, shared, jnp.where(eye, diagonal, turned))
    inverse = inverse_of(regular, eye, total, power)
    weights = exact(inverse, stack[b : 2 * b, :])
    coupled = stack[2 * b : 3 * b, :] - exact(squares, weights)
    correction = exact(inverse, coupled)
    weight_parts = jnp.concatenate(two_parts(weights), 1)
    correction_parts = jnp.concatenate(two_parts(correction), 1)
    copies = []

    def send(which, target, piece):
        part = slice(piece * rows, (piece + 1) * rows)
        copy = pltpu.make_async_copy(results.at[which, part], target.at[part], done.at[which, piece])
        copy.start()
        copies.append(copy)

    for piece in range(COPIES):
        part = slice(piece * rows, (piece + 1) * rows)
        product = dot(packed[part, :], weight_parts)
        results[0, part, :] = product[:, :b] + product[:, b:]
        send(0, solution, piece)
        moved = dot(upper[part, :], weight_parts)
        moved = moved[:, :b] + moved[:, b:] + dot(lower[part, :], weight_parts[:, :b])
        live = live_rows(scalars, piece * rows, rows, b)
        results[1, part, :] = jnp.where(live, rhs[part, :], 0.0) - moved
        send(1, residual, piece)
    for piece in range(COPIES):
        part = slice(piece * rows, (piece + 1) * rows)
        product = dot(packed[part, :], correction_parts)
        results[2, part, :] = results[1, part, :] - (product[:, :b] + product[:, b:])
        send(2, direction, piece)
    for copy in copies:
        copy.wait()


def factors(number):
    found, p = [], 2
    while number > 1:
        while number % p == 0:
            found.append(p)
            number //= p
        p += 1
    return found


def rounds_of(clusters, places):
    digits, stride = [], 2
    for radix in factors(places // 2) + factors(clusters):
        digits.append((stride, radix))
        stride *= radix
    groups = []
    for digit in digits:
        if groups and len(groups[-1]) == 1 and groups[-1][0][1] * digit[1] <= 4:
            groups[-1].append(digit)
        else:
            groups.append([digit])

    def moves(group):
        offsets = itertools.product(*[range(radix) for _, radix in reversed(group)])
        return [list(zip(reversed(group), o)) for o in offsets if any(o)]

    def moved(index, move):
        for (stride, radix), offset in move:
            digit = index // stride % radix
            index += ((digit + offset) % radix - digit) * stride
        return index

    forward = [moves(g) for g in groups]
    backward = forward[::-1]
    if [len(m) for m in forward] != [len(m) for m in backward]:
        backward = forward
    count = clusters * places
    return [
        [
            [(i, moved(i, (first, second)[i % 2])) for i in range(count)]
            for first, second in zip(ours, others)
        ]
        for ours, others in zip(forward, backward)
    ]


def per_device(clusters, places, operator, rhs, interface_sizes, neighbour_rows, kept_columns):
    matrix, right_side = operator[0], rhs[0]
    height, breadth = right_side.shape
    place = lax.axis_index("clu")
    core = lax.axis_index("sub") % 2
    scalars = jnp.stack(
        [interface_sizes[0], place, jnp.int32(clusters - 1), core]
    ).astype(jnp.int32)
    pairing = neighbour_rows.reshape(height // breadth, breadth)
    extra = 2 * pairing.shape[0]
    like = jax.ShapeDtypeStruct
    cost = pl.CostEstimate(
        flops=2 * height * height * breadth, bytes_accessed=2 * height * height, transcendentals=0
    )
    packed = pl.pallas_call(
        round_kernel,
        out_shape=like((height + extra, breadth), bf16),
        in_specs=[SMEM] + [HBM] * 3,
        out_specs=VMEM,
        scratch_shapes=[
            pltpu.VMEM((height, breadth), f32),
            pltpu.VMEM((1, breadth), jnp.int32),
            pltpu.VMEM(pairing.shape, jnp.int32),
            pltpu.SemaphoreType.DMA((3,)),
        ],
        compiler_params=parameters(),
        name="round",
    )(interface_sizes, *map(in_hbm, (right_side, kept_columns, pairing)))
    other = lax.ppermute(packed, "clu", [(i, i ^ 1) for i in range(clusters) if i ^ 1 < clusters])
    tile = min(height, 256)
    base = pl.pallas_call(
        local_kernel,
        grid=(height // tile,),
        out_shape=like((height, breadth), f32),
        in_specs=[SMEM, pl.BlockSpec((tile, height), lambda i: (i, 0)), VMEM],
        out_specs=VMEM,
        compiler_params=parameters(),
        cost_estimate=cost,
        name="local",
    )(scalars, in_hbm(matrix), packed)
    other, base = lax.optimization_barrier((other, base))
    onward = [(i, i + 2) for i in range(0, clusters - 2, 2)]
    onward += [(i, i - 2) for i in range(3, clusters, 2)]
    outside = lax.ppermute(other, "clu", onward)
    nearer = pl.pallas_call(
        near_kernel,
        out_shape=like((height, breadth), f32),
        in_specs=[SMEM] + [VMEM] * 3,
        out_specs=VMEM,
        compiler_params=parameters(),
        cost_estimate=cost,
        name="near",
    )(scalars, pairing, other, base)
    half = (3 * breadth + 16) // 2
    upper, lower, mine, theirs = pl.pallas_call(
        sums_kernel,
        out_shape=(
            like((height, breadth), bf16),
            like((height, breadth), bf16),
            like((half, breadth), f32),
            like((half, breadth), f32),
        ),
        in_specs=[SMEM] + [VMEM] * 5,
        out_specs=(VMEM,) * 4,
        scratch_shapes=[
            pltpu.VMEM((height, breadth), f32),
            pltpu.VMEM((2 * half, breadth), f32),
        ],
        compiler_params=parameters(),
        name="sums",
    )(scalars, pairing, outside, nearer, packed, right_side)
    swap = [(i, i ^ 1) for i in range(clusters * places)]
    mine = mine + lax.ppermute(theirs, AXES, swap)
    for routes in rounds_of(clusters, places):
        parts = [mine] + [lax.ppermute(mine, AXES, route) for route in routes]
        while len(parts) > 1:
            parts = [sum(parts[i : i + 2][1:], parts[i]) for i in range(0, len(parts), 2)]
        mine = parts[0]
    theirs = lax.ppermute(mine, AXES, swap)
    outs = pl.pallas_call(
        finish_kernel,
        out_shape=(like((height, breadth), f32),) * 3,
        in_specs=[SMEM] + [VMEM] * 7,
        out_specs=(HBM,) * 3,
        scratch_shapes=[
            pltpu.VMEM((2 * half, breadth), f32),
            pltpu.VMEM((breadth, breadth), f32),
            pltpu.VMEM((breadth, breadth), f32),
            pltpu.VMEM((3, height, breadth), f32),
            pltpu.SemaphoreType.DMA((3, COPIES)),
        ],
        compiler_params=parameters(),
        name="finish",
    )(scalars, kept_columns, mine, theirs, packed, upper, lower, right_side)
    return tuple(out[None] for out in outs)


def solution(mesh):
    clusters, places = mesh.shape["clu"], mesh.shape["sub"]
    return jax.shard_map(
        functools.partial(per_device, clusters, places),
        mesh=mesh,
        in_specs=(
            P(("clu", "sub"), None, None),
            P(("clu", "sub"), None, None),
            P(("clu", "sub")),
            P(("clu", "sub"), None),
            P(),
        ),
        out_specs=(P(("clu", "sub"), None, None),) * 3,
        check_vma=False,
    )
```

```python
import functools
import itertools

import jax
import jax.numpy as jnp
from jax import lax
from jax.experimental import pallas as pl
from jax.experimental.pallas import tpu as pltpu
from jax.sharding import PartitionSpec as P

stiffness = 1.0
f32 = jnp.float32
bf16 = jnp.bfloat16
AXES = ("clu", "sub")
VMEM_BYTES = 24 * 2**20
COPIES = 4
SMEM = pl.BlockSpec(memory_space=pltpu.SMEM)
VMEM = pl.BlockSpec(memory_space=pltpu.VMEM)
HBM = pl.BlockSpec(memory_space=pltpu.HBM)
SIZE, PLACE, LAST, CORE = range(4)


def dot(a, b):
    return jnp.dot(a, b, preferred_element_type=f32)


def exact(a, b):
    return jnp.dot(a, b, preferred_element_type=f32, precision=lax.Precision.HIGHEST)


def gram(a, b):
    return lax.dot_general(a, b, (((0,), (0,)), ((), ())), preferred_element_type=f32)


def two_parts(values):
    upper = values.astype(bf16)
    return upper, (values - upper.astype(f32)).astype(bf16)


def parameters():
    return pltpu.CompilerParams(vmem_limit_bytes=VMEM_BYTES)


def in_hbm(array):
    return pltpu.with_memory_space_constraint(array, pltpu.HBM)


def live_rows(scalars, start, rows, columns):
    return start + lax.broadcasted_iota(jnp.int32, (rows, columns), 0) < scalars[SIZE]


def round_kernel(sizes, rhs, kept, pairing, out, block, flags, rows, done):
    copies = [
        pltpu.make_async_copy(source, target, done.at[i])
        for i, (source, target) in enumerate(
            [(rhs, block), (kept, flags), (pairing, rows)]
        )
    ]
    for copy in copies:
        copy.start()
    for copy in copies:
        copy.wait()
    height, breadth = block.shape
    live = lax.broadcasted_iota(jnp.int32, (height, breadth), 0) < sizes[0]
    keep = flags[...].astype(f32)
    out[0:height, :] = (jnp.where(live, block[...], 0.0) * keep).astype(bf16)
    order = rows[...]
    digits = jnp.concatenate([order // 256, order % 256], 0)
    out[height:, :] = digits.astype(f32).astype(bf16)


def local_kernel(scalars, operator, packed, out):
    rows, height = operator.shape
    place = scalars[PLACE]
    degree = (place > 0).astype(f32) + (place < scalars[LAST]).astype(f32)
    here = pl.ds(pl.multiple_of(pl.program_id(0) * rows, rows), rows)
    own = packed[here, :].astype(f32)
    out[here, :] = dot(operator[...], packed[0:height, :]) + (stiffness * degree) * own


def picked(block, pairing, start, rows, inverse):
    count, lanes = pairing.shape
    strips = []
    if inverse:
        place = (start + lax.broadcasted_iota(jnp.int32, (rows, lanes), 0)).astype(f32)
        for k in range(count):
            strips.append(jnp.where(place == pairing[k : k + 1, :], 1.0, 0.0).astype(bf16))
        chosen = jnp.concatenate(strips, 1)
    else:
        column = lax.broadcasted_iota(jnp.int32, (lanes, lanes), 1).astype(f32)
        for first in range(start, start + rows, lanes):
            k = first // lanes
            wanted = jnp.broadcast_to(pairing[k : k + 1, :], (lanes, lanes)).T
            strips.append(
                jnp.concatenate(
                    [
                        jnp.where(wanted == column + float(j * lanes), 1.0, 0.0).astype(bf16)
                        for j in range(count)
                    ],
                    1,
                )
            )
        chosen = jnp.concatenate(strips, 0)
    return dot(chosen, block)


def sent_pairing(packed, height):
    digits = packed[height:, :].astype(f32)
    half = digits.shape[0] // 2
    return digits[:half] * 256.0 + digits[half:]


def near_kernel(scalars, pairing, other, base, out):
    height = base.shape[0]
    step = min(height, 256)
    even = scalars[PLACE] % 2 == 0

    def go(rows_of, inverse):
        for start in range(0, height, step):
            rows = slice(start, start + step)
            out[rows, :] = base[rows, :] - stiffness * picked(
                other[0:height, :], rows_of, start, step, inverse
            )

    @pl.when(even)
    def _():
        go(sent_pairing(other, height), True)

    @pl.when(jnp.logical_not(even))
    def _():
        go(pairing[...].astype(f32), False)


def sums_kernel(scalars, pairing, other, base, packed, rhs, upper, lower, mine, theirs, image, stack):
    height, breadth = base.shape
    step = min(height, 256)
    place = scalars[PLACE]
    even = place % 2 == 0
    outer = jnp.logical_or(place == 0, place == scalars[LAST])
    within = jnp.where(outer, 0.0, stiffness)

    def go(rows_of, inverse):
        for start in range(0, height, step):
            rows = slice(start, start + step)
            whole = base[rows, :] - within * picked(
                other[0:height, :], rows_of, start, step, inverse
            )
            image[rows, :] = jnp.where(live_rows(scalars, start, step, breadth), whole, 0.0)

    @pl.when(even)
    def _():
        go(pairing[...].astype(f32), False)

    @pl.when(jnp.logical_not(even))
    def _():
        go(sent_pairing(other, height), True)

    high, low = two_parts(image[...])
    upper[...] = high
    lower[...] = low
    residual = jnp.where(live_rows(scalars, 0, height, breadth), rhs[...], 0.0)
    res_high, res_low = two_parts(residual)
    right = jnp.concatenate([high, low, res_high, res_low], 1)
    first = gram(packed[0:height, :], right)
    second = gram(high, right)
    third = gram(low, res_high)
    b = breadth
    curvature = first[:, 0:b] + first[:, b : 2 * b]
    projected = first[:, 2 * b : 3 * b] + first[:, 3 * b :]
    mixed = second[:, b : 2 * b]
    squares = second[:, 0:b] + mixed + mixed.T
    cross = second[:, 2 * b : 3 * b] + second[:, 3 * b :] + third
    row = lax.broadcasted_iota(jnp.int32, (b, b), 0)
    column = lax.broadcasted_iota(jnp.int32, (b, b), 1)
    diagonal = jnp.sum(jnp.where(row == column, squares, 0.0), axis=0, keepdims=True)
    stack[0:b, :] = jnp.where(row >= column, curvature, squares)
    stack[b : 2 * b, :] = projected
    stack[2 * b : 3 * b, :] = cross
    stack[3 * b :, :] = jnp.broadcast_to(diagonal, (stack.shape[0] - 3 * b, b))
    half = mine.shape[0]
    core = scalars[CORE]
    mine[...] = stack[pl.ds(pl.multiple_of(core * half, 8), half), :]
    theirs[...] = stack[pl.ds(pl.multiple_of((1 - core) * half, 8), half), :]


def inverse_of(regular, eye, total, power):
    size = regular.shape[0]
    one = eye.astype(f32)
    kept = jnp.where(eye, regular, 0.0)
    scale_row = lax.rsqrt(jnp.sum(kept, axis=0, keepdims=True))
    scale_column = lax.rsqrt(jnp.sum(kept, axis=1, keepdims=True))
    scaled = regular * scale_row * scale_column
    error = one - scaled

    def factor(guess, now):
        both = exact(jnp.concatenate([guess, now], 0), now)
        return guess + both[:size], both[size:]

    guess, now = factor(*factor(one + error, exact(error, error)))
    total[...] = guess + exact(guess, now)

    @pl.when(jnp.logical_not(jnp.sum(now * now) < 1e-6))
    def _():
        c = 1.0 / jnp.max(jnp.sum(jnp.abs(scaled), axis=0, keepdims=True))
        smaller = one - c * scaled
        total[...] = c * (one + smaller)
        first = exact(smaller, smaller)
        power[...] = first

        def more(state):
            count, norm = state
            return jnp.logical_and(norm > 1e-6, count < 48)

        def again(state):
            guess, now = factor(total[...], power[...])
            total[...] = guess
            power[...] = now
            return state[0] + 1, jnp.sum(now * now)

        lax.while_loop(more, again, (jnp.int32(0), jnp.sum(first * first)))
        guess = total[...]
        total[...] = guess + exact(guess, one - exact(scaled, guess))

    return total[...] * scale_row * scale_column


def finish_kernel(
    scalars, kept, mine, theirs, packed, upper, lower, rhs, solution, residual, direction,
    stack, total, power, results, done,
):
    height, b = rhs.shape
    rows = results.shape[1] // COPIES
    half = mine.shape[0]
    core = scalars[CORE]
    stack[pl.ds(pl.multiple_of(core * half, 8), half), :] = mine[...]
    stack[pl.ds(pl.multiple_of((1 - core) * half, 8), half), :] = theirs[...]
    keep = kept[...].astype(f32)
    row = lax.broadcasted_iota(jnp.int32, (b, b), 0)
    column = lax.broadcasted_iota(jnp.int32, (b, b), 1)
    eye = row == column
    shared = stack[0:b, :]
    turned = shared.T
    regular = jnp.where(row >= column, shared, turned)
    regular = regular + jnp.where(eye, jnp.broadcast_to(1.0 - keep, (b, b)), 0.0)
    diagonal = jnp.broadcast_to(stack[3 * b : 3 * b + 1, :], (b, b))
    squares = jnp.where(row < column, shared, jnp.where(eye, diagonal, turned))
    inverse = inverse_of(regular, eye, total, power)
    weights = exact(inverse, stack[b : 2 * b, :])
    coupled = stack[2 * b : 3 * b, :] - exact(squares, weights)
    correction = exact(inverse, coupled)
    weight_parts = jnp.concatenate(two_parts(weights), 1)
    correction_parts = jnp.concatenate(two_parts(correction), 1)
    copies = []

    def send(which, target, piece):
        part = slice(piece * rows, (piece + 1) * rows)
        copy = pltpu.make_async_copy(results.at[which, part], target.at[part], done.at[which, piece])
        copy.start()
        copies.append(copy)

    for piece in range(COPIES):
        part = slice(piece * rows, (piece + 1) * rows)
        product = dot(packed[part, :], weight_parts)
        results[0, part, :] = product[:, :b] + product[:, b:]
        send(0, solution, piece)
        moved = dot(upper[part, :], weight_parts)
        moved = moved[:, :b] + moved[:, b:] + dot(lower[part, :], weight_parts[:, :b])
        live = live_rows(scalars, piece * rows, rows, b)
        results[1, part, :] = jnp.where(live, rhs[part, :], 0.0) - moved
        send(1, residual, piece)
    for piece in range(COPIES):
        part = slice(piece * rows, (piece + 1) * rows)
        product = dot(packed[part, :], correction_parts)
        results[2, part, :] = results[1, part, :] - (product[:, :b] + product[:, b:])
        send(2, direction, piece)
    for copy in copies:
        copy.wait()


def factors(number):
    found, p = [], 2
    while number > 1:
        while number % p == 0:
            found.append(p)
            number //= p
        p += 1
    return found


def rounds_of(clusters, places):
    digits, stride = [], 2
    for radix in factors(places // 2) + factors(clusters):
        digits.append((stride, radix))
        stride *= radix
    groups = []
    for digit in digits:
        if groups and len(groups[-1]) == 1 and groups[-1][0][1] * digit[1] <= 4:
            groups[-1].append(digit)
        else:
            groups.append([digit])

    def moves(group):
        offsets = itertools.product(*[range(radix) for _, radix in reversed(group)])
        return [list(zip(reversed(group), o)) for o in offsets if any(o)]

    def moved(index, move):
        for (stride, radix), offset in move:
            digit = index // stride % radix
            index += ((digit + offset) % radix - digit) * stride
        return index

    forward = [moves(g) for g in groups]
    backward = forward[::-1]
    if [len(m) for m in forward] != [len(m) for m in backward]:
        backward = forward
    count = clusters * places
    return [
        [
            [(i, moved(i, (first, second)[i % 2])) for i in range(count)]
            for first, second in zip(ours, others)
        ]
        for ours, others in zip(forward, backward)
    ]


def per_device(clusters, places, operator, rhs, interface_sizes, neighbour_rows, kept_columns):
    matrix, right_side = operator[0], rhs[0]
    height, breadth = right_side.shape
    place = lax.axis_index("clu")
    core = lax.axis_index("sub") % 2
    scalars = jnp.stack(
        [interface_sizes[0], place, jnp.int32(clusters - 1), core]
    ).astype(jnp.int32)
    pairing = neighbour_rows.reshape(height // breadth, breadth)
    extra = 2 * pairing.shape[0]
    like = jax.ShapeDtypeStruct
    cost = pl.CostEstimate(
        flops=2 * height * height * breadth, bytes_accessed=2 * height * height, transcendentals=0
    )
    packed = pl.pallas_call(
        round_kernel,
        out_shape=like((height + extra, breadth), bf16),
        in_specs=[SMEM] + [HBM] * 3,
        out_specs=VMEM,
        scratch_shapes=[
            pltpu.VMEM((height, breadth), f32),
            pltpu.VMEM((1, breadth), jnp.int32),
            pltpu.VMEM(pairing.shape, jnp.int32),
            pltpu.SemaphoreType.DMA((3,)),
        ],
        compiler_params=parameters(),
        name="round",
    )(interface_sizes, *map(in_hbm, (right_side, kept_columns, pairing)))
    other = lax.ppermute(packed, "clu", [(i, i ^ 1) for i in range(clusters) if i ^ 1 < clusters])
    tile = min(height, 256)
    base = pl.pallas_call(
        local_kernel,
        grid=(height // tile,),
        out_shape=like((height, breadth), f32),
        in_specs=[SMEM, pl.BlockSpec((tile, height), lambda i: (i, 0)), VMEM],
        out_specs=VMEM,
        compiler_params=parameters(),
        cost_estimate=cost,
        name="local",
    )(scalars, in_hbm(matrix), packed)
    other, base = lax.optimization_barrier((other, base))
    onward = [(i, i + 2 if i + 2 < clusters else i + 1) for i in range(0, clusters, 2)]
    onward += [(i, max(i - 2, 0)) for i in range(1, clusters, 2)]
    outside = lax.ppermute(other, "clu", onward)
    nearer = pl.pallas_call(
        near_kernel,
        out_shape=like((height, breadth), f32),
        in_specs=[SMEM] + [VMEM] * 3,
        out_specs=VMEM,
        compiler_params=parameters(),
        cost_estimate=cost,
        name="near",
    )(scalars, pairing, other, base)
    half = (3 * breadth + 16) // 2
    upper, lower, mine, theirs = pl.pallas_call(
        sums_kernel,
        out_shape=(
            like((height, breadth), bf16),
            like((height, breadth), bf16),
            like((half, breadth), f32),
            like((half, breadth), f32),
        ),
        in_specs=[SMEM] + [VMEM] * 5,
        out_specs=(VMEM,) * 4,
        scratch_shapes=[
            pltpu.VMEM((height, breadth), f32),
            pltpu.VMEM((2 * half, breadth), f32),
        ],
        compiler_params=parameters(),
        name="sums",
    )(scalars, pairing, outside, nearer, packed, right_side)
    swap = [(i, i ^ 1) for i in range(clusters * places)]
    mine = mine + lax.ppermute(theirs, AXES, swap)
    for routes in rounds_of(clusters, places):
        parts = [mine] + [lax.ppermute(mine, AXES, route) for route in routes]
        while len(parts) > 1:
            parts = [sum(parts[i : i + 2][1:], parts[i]) for i in range(0, len(parts), 2)]
        mine = parts[0]
    theirs = lax.ppermute(mine, AXES, swap)
    outs = pl.pallas_call(
        finish_kernel,
        out_shape=(like((height, breadth), f32),) * 3,
        in_specs=[SMEM] + [VMEM] * 7,
        out_specs=(HBM,) * 3,
        scratch_shapes=[
            pltpu.VMEM((2 * half, breadth), f32),
            pltpu.VMEM((breadth, breadth), f32),
            pltpu.VMEM((breadth, breadth), f32),
            pltpu.VMEM((3, height, breadth), f32),
            pltpu.SemaphoreType.DMA((3, COPIES)),
        ],
        compiler_params=parameters(),
        name="finish",
    )(scalars, kept_columns, mine, theirs, packed, upper, lower, right_side)
    return tuple(out[None] for out in outs)


def solution(mesh):
    clusters, places = mesh.shape["clu"], mesh.shape["sub"]
    return jax.shard_map(
        functools.partial(per_device, clusters, places),
        mesh=mesh,
        in_specs=(
            P(("clu", "sub"), None, None),
            P(("clu", "sub"), None, None),
            P(("clu", "sub")),
            P(("clu", "sub"), None),
            P(),
        ),
        out_specs=(P(("clu", "sub"), None, None),) * 3,
        check_vma=False,
    )
```

```python
import functools
import itertools

import jax
import jax.numpy as jnp
from jax import lax
from jax.experimental import pallas as pl
from jax.experimental.pallas import tpu as pltpu
from jax.sharding import PartitionSpec as P

stiffness = 1.0
f32 = jnp.float32
bf16 = jnp.bfloat16
AXES = ("clu", "sub")
VMEM_BYTES = 24 * 2**20
COPIES = 4
PIECES = 1
SMEM = pl.BlockSpec(memory_space=pltpu.SMEM)
VMEM = pl.BlockSpec(memory_space=pltpu.VMEM)
HBM = pl.BlockSpec(memory_space=pltpu.HBM)
SIZE, PLACE, LAST, CORE = range(4)


def dot(a, b):
    return jnp.dot(a, b, preferred_element_type=f32)


def exact(a, b):
    return jnp.dot(a, b, preferred_element_type=f32, precision=lax.Precision.HIGHEST)


def nearly(a, b):
    columns = b.shape[1]
    a_high, a_low = two_parts(a)
    b_high, b_low = two_parts(b)
    first = dot(a_high, jnp.concatenate([b_high, b_low], 1))
    return first[:, :columns] + first[:, columns:] + dot(a_low, b_high)


def gram(a, b):
    return lax.dot_general(a, b, (((0,), (0,)), ((), ())), preferred_element_type=f32)


def two_parts(values):
    upper = values.astype(bf16)
    return upper, (values - upper.astype(f32)).astype(bf16)


def parameters():
    return pltpu.CompilerParams(vmem_limit_bytes=VMEM_BYTES)


def in_hbm(array):
    return pltpu.with_memory_space_constraint(array, pltpu.HBM)


def live_rows(scalars, start, rows, columns):
    return start + lax.broadcasted_iota(jnp.int32, (rows, columns), 0) < scalars[SIZE]


def round_kernel(sizes, rhs, kept, pairing, *refs):
    outs, (listed, block, flags, rows, done) = refs[:PIECES], refs[PIECES:]
    copies = [
        pltpu.make_async_copy(source, target, done.at[i])
        for i, (source, target) in enumerate(
            [(rhs, block), (kept, flags), (pairing, rows)]
        )
    ]
    for copy in copies:
        copy.start()
    for copy in copies:
        copy.wait()
    height, breadth = block.shape
    live = lax.broadcasted_iota(jnp.int32, (height, breadth), 0) < sizes[0]
    keep = flags[...].astype(f32)
    rounded = (jnp.where(live, block[...], 0.0) * keep).astype(bf16)
    step = height // PIECES
    for i, out in enumerate(outs):
        out[0:step, :] = rounded[i * step : (i + 1) * step]
    order = rows[...]
    listed[...] = order.astype(f32)
    digits = jnp.concatenate([order // 256, order % 256], 0)
    outs[-1][step:, :] = digits.astype(f32).astype(bf16)


def picked(block, pairing, start, rows, inverse):
    count, lanes = pairing.shape
    strips = []
    if inverse:
        place = (start + lax.broadcasted_iota(jnp.int32, (rows, lanes), 0)).astype(f32)
        for k in range(count):
            strips.append(jnp.where(place == pairing[k : k + 1, :], 1.0, 0.0).astype(bf16))
        chosen = jnp.concatenate(strips, 1)
    else:
        column = lax.broadcasted_iota(jnp.int32, (lanes, lanes), 1).astype(f32)
        for first in range(start, start + rows, lanes):
            k = first // lanes
            wanted = jnp.broadcast_to(pairing[k : k + 1, :], (lanes, lanes)).T
            strips.append(
                jnp.concatenate(
                    [
                        jnp.where(wanted == column + float(j * lanes), 1.0, 0.0).astype(bf16)
                        for j in range(count)
                    ],
                    1,
                )
            )
        chosen = jnp.concatenate(strips, 0)
    return dot(chosen, block)


def joined(pieces, height):
    step = height // PIECES
    return jnp.concatenate([piece[0:step, :] for piece in pieces], 0)


def sent_pairing(pieces, height):
    digits = pieces[-1][height // PIECES :, :].astype(f32)
    half = digits.shape[0] // 2
    return digits[:half] * 256.0 + digits[half:]


def local_kernel(scalars, operator, *refs):
    own, (out, matrix, done) = refs[:PIECES], refs[PIECES:]
    height = out.shape[0]
    step = min(height, 256)
    strips = [slice(start, start + step) for start in range(0, height, step)]
    copies = [
        pltpu.make_async_copy(operator.at[rows], matrix.at[rows], done.at[i])
        for i, rows in enumerate(strips)
    ]
    for copy in copies:
        copy.start()
    place = scalars[PLACE]
    degree = (place > 0).astype(f32) + (place < scalars[LAST]).astype(f32)
    block = joined(own, height)
    for rows, copy in zip(strips, copies):
        copy.wait()
        out[rows, :] = dot(matrix[rows, :], block) + (stiffness * degree) * block[rows].astype(f32)


def near_kernel(scalars, pairing, base, *refs):
    other, out = refs[:PIECES], refs[PIECES]
    height = out.shape[0]
    step = min(height, 256)
    even = scalars[PLACE] % 2 == 0

    def go(rows_of, inverse):
        block = joined(other, height)
        for start in range(0, height, step):
            rows = slice(start, start + step)
            out[rows, :] = base[rows, :] - stiffness * picked(block, rows_of, start, step, inverse)

    @pl.when(even)
    def _():
        go(sent_pairing(other, height), True)

    @pl.when(jnp.logical_not(even))
    def _():
        go(pairing[...], False)


def sums_kernel(scalars, pairing, base, rhs, *refs):
    other, own = refs[:PIECES], refs[PIECES : 2 * PIECES]
    upper, lower, mine, theirs, image, stack = refs[2 * PIECES :]
    height, breadth = base.shape
    step = min(height, 256)
    place = scalars[PLACE]
    even = place % 2 == 0
    outer = jnp.logical_or(place == 0, place == scalars[LAST])
    within = jnp.where(outer, 0.0, stiffness)

    def go(rows_of, inverse):
        block = joined(other, height)
        for start in range(0, height, step):
            rows = slice(start, start + step)
            whole = base[rows, :] - within * picked(block, rows_of, start, step, inverse)
            image[rows, :] = jnp.where(live_rows(scalars, start, step, breadth), whole, 0.0)

    @pl.when(even)
    def _():
        go(pairing[...], False)

    @pl.when(jnp.logical_not(even))
    def _():
        go(sent_pairing(other, height), True)

    high, low = two_parts(image[...])
    upper[...] = high
    lower[...] = low
    residual = jnp.where(live_rows(scalars, 0, height, breadth), rhs[...], 0.0)
    res_high, res_low = two_parts(residual)
    right = jnp.concatenate([high, low, res_high, res_low], 1)
    first = gram(joined(own, height), right)
    second = gram(high, right)
    third = gram(low, res_high)
    b = breadth
    curvature = first[:, 0:b] + first[:, b : 2 * b]
    projected = first[:, 2 * b : 3 * b] + first[:, 3 * b :]
    mixed = second[:, b : 2 * b]
    squares = second[:, 0:b] + mixed + mixed.T
    cross = second[:, 2 * b : 3 * b] + second[:, 3 * b :] + third
    row = lax.broadcasted_iota(jnp.int32, (b, b), 0)
    column = lax.broadcasted_iota(jnp.int32, (b, b), 1)
    diagonal = jnp.sum(jnp.where(row == column, squares, 0.0), axis=0, keepdims=True)
    stack[0:b, :] = jnp.where(row >= column, curvature, squares)
    stack[b : 2 * b, :] = projected
    stack[2 * b : 3 * b, :] = cross
    stack[3 * b :, :] = jnp.broadcast_to(diagonal, (stack.shape[0] - 3 * b, b))
    half = mine.shape[0]
    core = scalars[CORE]
    mine[...] = stack[pl.ds(pl.multiple_of(core * half, 8), half), :]
    theirs[...] = stack[pl.ds(pl.multiple_of((1 - core) * half, 8), half), :]


def inverse_of(regular, eye, total, power):
    size = regular.shape[0]
    one = eye.astype(f32)
    kept = jnp.where(eye, regular, 0.0)
    scale_row = lax.rsqrt(jnp.sum(kept, axis=0, keepdims=True))
    scale_column = lax.rsqrt(jnp.sum(kept, axis=1, keepdims=True))
    scaled = regular * scale_row * scale_column
    error = one - scaled

    def factor(guess, now, product):
        both = product(jnp.concatenate([guess, now], 0), now)
        return guess + both[:size], both[size:]

    guess, now = factor(one + error, nearly(error, error), nearly)
    guess, now = factor(guess, now, nearly)
    total[...] = guess + nearly(guess, now)

    @pl.when(jnp.logical_not(jnp.sum(now * now) < 1e-6))
    def _():
        c = 1.0 / jnp.max(jnp.sum(jnp.abs(scaled), axis=0, keepdims=True))
        smaller = one - c * scaled
        total[...] = c * (one + smaller)
        first = exact(smaller, smaller)
        power[...] = first

        def more(state):
            count, norm = state
            return jnp.logical_and(norm > 1e-6, count < 48)

        def again(state):
            guess, now = factor(total[...], power[...], exact)
            total[...] = guess
            power[...] = now
            return state[0] + 1, jnp.sum(now * now)

        lax.while_loop(more, again, (jnp.int32(0), jnp.sum(first * first)))
        guess = total[...]
        total[...] = guess + exact(guess, one - exact(scaled, guess))

    return total[...] * scale_row * scale_column


def finish_kernel(
    scalars, kept, mine, theirs, upper, lower, rhs, *refs
):
    own, (solution, residual, direction) = refs[:PIECES], refs[PIECES : PIECES + 3]
    stack, total, power, results, done = refs[PIECES + 3 :]
    height, b = rhs.shape
    rows = results.shape[1] // COPIES
    half = mine.shape[0]
    core = scalars[CORE]
    stack[pl.ds(pl.multiple_of(core * half, 8), half), :] = mine[...]
    stack[pl.ds(pl.multiple_of((1 - core) * half, 8), half), :] = theirs[...]
    keep = kept[...].astype(f32)
    row = lax.broadcasted_iota(jnp.int32, (b, b), 0)
    column = lax.broadcasted_iota(jnp.int32, (b, b), 1)
    eye = row == column
    shared = stack[0:b, :]
    turned = shared.T
    regular = jnp.where(row >= column, shared, turned)
    regular = regular + jnp.where(eye, jnp.broadcast_to(1.0 - keep, (b, b)), 0.0)
    diagonal = jnp.broadcast_to(stack[3 * b : 3 * b + 1, :], (b, b))
    squares = jnp.where(row < column, shared, jnp.where(eye, diagonal, turned))
    inverse = inverse_of(regular, eye, total, power)
    weights = exact(inverse, stack[b : 2 * b, :])
    coupled = stack[2 * b : 3 * b, :] - exact(squares, weights)
    correction = exact(inverse, coupled)
    weight_parts = jnp.concatenate(two_parts(weights), 1)
    correction_parts = jnp.concatenate(two_parts(correction), 1)
    packed = joined(own, height)
    copies = []

    def send(which, target, piece):
        part = slice(piece * rows, (piece + 1) * rows)
        copy = pltpu.make_async_copy(results.at[which, part], target.at[part], done.at[which, piece])
        copy.start()
        copies.append(copy)

    for piece in range(COPIES):
        part = slice(piece * rows, (piece + 1) * rows)
        product = dot(packed[part], weight_parts)
        results[0, part, :] = product[:, :b] + product[:, b:]
        send(0, solution, piece)
        moved = dot(upper[part, :], weight_parts)
        moved = moved[:, :b] + moved[:, b:] + dot(lower[part, :], weight_parts[:, :b])
        live = live_rows(scalars, piece * rows, rows, b)
        results[1, part, :] = jnp.where(live, rhs[part, :], 0.0) - moved
        send(1, residual, piece)
    for piece in range(COPIES):
        part = slice(piece * rows, (piece + 1) * rows)
        product = dot(packed[part], correction_parts)
        results[2, part, :] = results[1, part, :] - (product[:, :b] + product[:, b:])
        send(2, direction, piece)
    for copy in copies:
        copy.wait()


def factors(number):
    found, p = [], 2
    while number > 1:
        while number % p == 0:
            found.append(p)
            number //= p
        p += 1
    return found


def rounds_of(clusters, places):
    digits, stride = [], 2
    for radix in factors(places // 2) + factors(clusters):
        digits.append((stride, radix))
        stride *= radix
    groups = []
    for digit in digits:
        if groups and len(groups[-1]) == 1 and groups[-1][0][1] * digit[1] <= 4:
            groups[-1].append(digit)
        else:
            groups.append([digit])

    def moves(group):
        offsets = itertools.product(*[range(radix) for _, radix in reversed(group)])
        return [list(zip(reversed(group), o)) for o in offsets if any(o)]

    def moved(index, move):
        for (stride, radix), offset in move:
            digit = index // stride % radix
            index += ((digit + offset) % radix - digit) * stride
        return index

    forward = [moves(g) for g in groups]
    backward = forward[::-1]
    if [len(m) for m in forward] != [len(m) for m in backward]:
        backward = forward
    count = clusters * places
    return [
        [
            [(i, moved(i, (first, second)[i % 2])) for i in range(count)]
            for first, second in zip(ours, others)
        ]
        for ours, others in zip(forward, backward)
    ]


def per_device(clusters, places, operator, rhs, interface_sizes, neighbour_rows, kept_columns):
    matrix, right_side = operator[0], rhs[0]
    height, breadth = right_side.shape
    place = lax.axis_index("clu")
    core = lax.axis_index("sub") % 2
    scalars = jnp.stack(
        [interface_sizes[0], place, jnp.int32(clusters - 1), core]
    ).astype(jnp.int32)
    pairing = neighbour_rows.reshape(height // breadth, breadth)
    extra = 2 * pairing.shape[0]
    like = jax.ShapeDtypeStruct
    cost = pl.CostEstimate(
        flops=2 * height * height * breadth, bytes_accessed=2 * height * height, transcendentals=0
    )
    piece = height // PIECES
    shapes = [like((piece, breadth), bf16)] * (PIECES - 1) + [like((piece + extra, breadth), bf16)]
    *packed, listed = pl.pallas_call(
        round_kernel,
        out_shape=(*shapes, like(pairing.shape, f32)),
        in_specs=[SMEM] + [HBM] * 3,
        out_specs=(VMEM,) * (PIECES + 1),
        scratch_shapes=[
            pltpu.VMEM((height, breadth), f32),
            pltpu.VMEM((1, breadth), jnp.int32),
            pltpu.VMEM(pairing.shape, jnp.int32),
            pltpu.SemaphoreType.DMA((3,)),
        ],
        compiler_params=parameters(),
        name="round",
    )(interface_sizes, *map(in_hbm, (right_side, kept_columns, pairing)))
    pairs = [(i, i ^ 1) for i in range(clusters)]
    other = [lax.ppermute(part, "clu", pairs) for part in packed]
    strips = height // min(height, 256)
    base = pl.pallas_call(
        local_kernel,
        out_shape=like((height, breadth), f32),
        in_specs=[SMEM, HBM] + [VMEM] * PIECES,
        out_specs=VMEM,
        scratch_shapes=[pltpu.VMEM((height, height), bf16), pltpu.SemaphoreType.DMA((strips,))],
        compiler_params=parameters(),
        cost_estimate=cost,
        name="local",
    )(scalars, in_hbm(matrix), *packed)
    other[0], base = lax.optimization_barrier((other[0], base))
    onward = [(i, i + 2 if i + 2 < clusters else i + 1) for i in range(0, clusters, 2)]
    onward += [(i, max(i - 2, 0)) for i in range(1, clusters, 2)]
    outside = [lax.ppermute(part, "clu", onward) for part in other]
    nearer = pl.pallas_call(
        near_kernel,
        out_shape=like((height, breadth), f32),
        in_specs=[SMEM] + [VMEM] * (2 + PIECES),
        out_specs=VMEM,
        compiler_params=parameters(),
        cost_estimate=cost,
        name="near",
    )(scalars, listed, base, *other)
    half = (3 * breadth + 16) // 2
    upper, lower, mine, theirs = pl.pallas_call(
        sums_kernel,
        out_shape=(
            like((height, breadth), bf16),
            like((height, breadth), bf16),
            like((half, breadth), f32),
            like((half, breadth), f32),
        ),
        in_specs=[SMEM] + [VMEM] * (3 + 2 * PIECES),
        out_specs=(VMEM,) * 4,
        scratch_shapes=[
            pltpu.VMEM((height, breadth), f32),
            pltpu.VMEM((2 * half, breadth), f32),
        ],
        compiler_params=parameters(),
        name="sums",
    )(scalars, listed, nearer, right_side, *outside, *packed)
    swap = [(i, i ^ 1) for i in range(clusters * places)]
    mine = mine + lax.ppermute(theirs, AXES, swap)
    for routes in rounds_of(clusters, places):
        parts = [mine] + [lax.ppermute(mine, AXES, route) for route in routes]
        while len(parts) > 1:
            parts = [sum(parts[i : i + 2][1:], parts[i]) for i in range(0, len(parts), 2)]
        mine = parts[0]
    theirs = lax.ppermute(mine, AXES, swap)
    outs = pl.pallas_call(
        finish_kernel,
        out_shape=(like((height, breadth), f32),) * 3,
        in_specs=[SMEM] + [VMEM] * (6 + PIECES),
        out_specs=(HBM,) * 3,
        scratch_shapes=[
            pltpu.VMEM((2 * half, breadth), f32),
            pltpu.VMEM((breadth, breadth), f32),
            pltpu.VMEM((breadth, breadth), f32),
            pltpu.VMEM((3, height, breadth), f32),
            pltpu.SemaphoreType.DMA((3, COPIES)),
        ],
        compiler_params=parameters(),
        name="finish",
    )(scalars, kept_columns, mine, theirs, upper, lower, right_side, *packed)
    return tuple(out[None] for out in outs)


def solution(mesh):
    clusters, places = mesh.shape["clu"], mesh.shape["sub"]
    return jax.shard_map(
        functools.partial(per_device, clusters, places),
        mesh=mesh,
        in_specs=(
            P(("clu", "sub"), None, None),
            P(("clu", "sub"), None, None),
            P(("clu", "sub")),
            P(("clu", "sub"), None),
            P(),
        ),
        out_specs=(P(("clu", "sub"), None, None),) * 3,
        check_vma=False,
    )
```

```python
import functools
import itertools

import jax
import jax.numpy as jnp
from jax import lax
from jax.experimental import pallas as pl
from jax.experimental.pallas import tpu as pltpu
from jax.sharding import PartitionSpec as P

stiffness = 1.0
f32 = jnp.float32
bf16 = jnp.bfloat16
AXES = ("clu", "sub")
VMEM_BYTES = 24 * 2**20
COPIES = 4
PIECES = 1
SMEM = pl.BlockSpec(memory_space=pltpu.SMEM)
VMEM = pl.BlockSpec(memory_space=pltpu.VMEM)
HBM = pl.BlockSpec(memory_space=pltpu.HBM)
SIZE, PLACE, LAST, CORE = range(4)


def dot(a, b):
    return jnp.dot(a, b, preferred_element_type=f32)


def exact(a, b):
    return jnp.dot(a, b, preferred_element_type=f32, precision=lax.Precision.HIGHEST)


def nearly(a, b):
    columns = b.shape[1]
    a_high, a_low = two_parts(a)
    b_high, b_low = two_parts(b)
    first = dot(a_high, jnp.concatenate([b_high, b_low], 1))
    return first[:, :columns] + first[:, columns:] + dot(a_low, b_high)


def gram(a, b):
    return lax.dot_general(a, b, (((0,), (0,)), ((), ())), preferred_element_type=f32)


def two_parts(values):
    upper = values.astype(bf16)
    return upper, (values - upper.astype(f32)).astype(bf16)


def parameters():
    return pltpu.CompilerParams(vmem_limit_bytes=VMEM_BYTES)


def in_hbm(array):
    return pltpu.with_memory_space_constraint(array, pltpu.HBM)


def live_rows(scalars, start, rows, columns):
    return start + lax.broadcasted_iota(jnp.int32, (rows, columns), 0) < scalars[SIZE]


def round_kernel(sizes, rhs, kept, pairing, *refs):
    outs, (listed, block, flags, rows, done) = refs[:PIECES], refs[PIECES:]
    copies = [
        pltpu.make_async_copy(source, target, done.at[i])
        for i, (source, target) in enumerate(
            [(rhs, block), (kept, flags), (pairing, rows)]
        )
    ]
    for copy in copies:
        copy.start()
    for copy in copies:
        copy.wait()
    height, breadth = block.shape
    live = lax.broadcasted_iota(jnp.int32, (height, breadth), 0) < sizes[0]
    keep = flags[...].astype(f32)
    rounded = (jnp.where(live, block[...], 0.0) * keep).astype(bf16)
    step = height // PIECES
    for i, out in enumerate(outs):
        out[0:step, :] = rounded[i * step : (i + 1) * step]
    order = rows[...]
    listed[...] = order.astype(f32)
    digits = jnp.concatenate([order // 256, order % 256], 0)
    outs[-1][step:, :] = digits.astype(f32).astype(bf16)


def picked(block, pairing, start, rows, inverse):
    count, lanes = pairing.shape
    strips = []
    if inverse:
        place = (start + lax.broadcasted_iota(jnp.int32, (rows, lanes), 0)).astype(f32)
        for k in range(count):
            strips.append(jnp.where(place == pairing[k : k + 1, :], 1.0, 0.0).astype(bf16))
        chosen = jnp.concatenate(strips, 1)
    else:
        column = lax.broadcasted_iota(jnp.int32, (lanes, lanes), 1).astype(f32)
        for first in range(start, start + rows, lanes):
            k = first // lanes
            wanted = jnp.broadcast_to(pairing[k : k + 1, :], (lanes, lanes)).T
            strips.append(
                jnp.concatenate(
                    [
                        jnp.where(wanted == column + float(j * lanes), 1.0, 0.0).astype(bf16)
                        for j in range(count)
                    ],
                    1,
                )
            )
        chosen = jnp.concatenate(strips, 0)
    return dot(chosen, block)


def joined(pieces, height):
    step = height // PIECES
    return jnp.concatenate([piece[0:step, :] for piece in pieces], 0)


def sent_pairing(pieces, height):
    digits = pieces[-1][height // PIECES :, :].astype(f32)
    half = digits.shape[0] // 2
    return digits[:half] * 256.0 + digits[half:]


def local_kernel(scalars, operator, *refs):
    own, (out, matrix, done) = refs[:PIECES], refs[PIECES:]
    height = out.shape[0]
    step = min(height, 256)
    strips = [slice(start, start + step) for start in range(0, height, step)]
    copies = [
        pltpu.make_async_copy(operator.at[rows], matrix.at[rows], done.at[i])
        for i, rows in enumerate(strips)
    ]
    for copy in copies:
        copy.start()
    place = scalars[PLACE]
    degree = (place > 0).astype(f32) + (place < scalars[LAST]).astype(f32)
    block = joined(own, height)
    for rows, copy in zip(strips, copies):
        copy.wait()
        out[rows, :] = dot(matrix[rows, :], block) + (stiffness * degree) * block[rows].astype(f32)


def near_kernel(scalars, pairing, base, rhs, *refs):
    other, own = refs[:PIECES], refs[PIECES : 2 * PIECES]
    out, turned, parts, projected = refs[2 * PIECES :]
    height, breadth = rhs.shape
    residual = jnp.where(live_rows(scalars, 0, height, breadth), rhs[...], 0.0)
    halves = jnp.concatenate(two_parts(residual), 1)
    parts[...] = halves
    flat = joined(own, height).T
    turned[...] = flat
    both = dot(flat, halves)
    projected[...] = both[:, :breadth] + both[:, breadth:]
    step = min(height, 256)
    even = scalars[PLACE] % 2 == 0

    def go(rows_of, inverse):
        block = joined(other, height)
        for start in range(0, height, step):
            rows = slice(start, start + step)
            out[rows, :] = base[rows, :] - stiffness * picked(block, rows_of, start, step, inverse)

    @pl.when(even)
    def _():
        go(sent_pairing(other, height), True)

    @pl.when(jnp.logical_not(even))
    def _():
        go(pairing[...], False)


def sums_kernel(scalars, pairing, base, turned, parts, projected, *refs):
    other, (upper, lower, mine, theirs, image, stack) = refs[:PIECES], refs[PIECES:]
    height, breadth = base.shape
    step = min(height, 256)
    place = scalars[PLACE]
    even = place % 2 == 0
    outer = jnp.logical_or(place == 0, place == scalars[LAST])
    within = jnp.where(outer, 0.0, stiffness)

    def go(rows_of, inverse):
        block = joined(other, height)
        for start in range(0, height, step):
            rows = slice(start, start + step)
            whole = base[rows, :] - within * picked(block, rows_of, start, step, inverse)
            image[rows, :] = jnp.where(live_rows(scalars, start, step, breadth), whole, 0.0)

    @pl.when(even)
    def _():
        go(pairing[...], False)

    @pl.when(jnp.logical_not(even))
    def _():
        go(sent_pairing(other, height), True)

    high, low = two_parts(image[...])
    upper[...] = high
    lower[...] = low
    split = jnp.concatenate([high, low], 1)
    first = dot(turned[...], split)
    second = gram(high, jnp.concatenate([split, parts[...]], 1))
    third = gram(low, parts[:, 0:breadth])
    b = breadth
    curvature = first[:, 0:b] + first[:, b : 2 * b]
    mixed = second[:, b : 2 * b]
    squares = second[:, 0:b] + mixed + mixed.T
    cross = second[:, 2 * b : 3 * b] + second[:, 3 * b :] + third
    row = lax.broadcasted_iota(jnp.int32, (b, b), 0)
    column = lax.broadcasted_iota(jnp.int32, (b, b), 1)
    diagonal = jnp.sum(jnp.where(row == column, squares, 0.0), axis=0, keepdims=True)
    stack[0:b, :] = jnp.where(row >= column, curvature, squares)
    stack[b : 2 * b, :] = projected[...]
    stack[2 * b : 3 * b, :] = cross
    stack[3 * b :, :] = jnp.broadcast_to(diagonal, (stack.shape[0] - 3 * b, b))
    half = mine.shape[0]
    core = scalars[CORE]
    mine[...] = stack[pl.ds(pl.multiple_of(core * half, 8), half), :]
    theirs[...] = stack[pl.ds(pl.multiple_of((1 - core) * half, 8), half), :]


def inverse_of(regular, eye, total, power):
    size = regular.shape[0]
    one = eye.astype(f32)
    kept = jnp.where(eye, regular, 0.0)
    scale_row = lax.rsqrt(jnp.sum(kept, axis=0, keepdims=True))
    scale_column = lax.rsqrt(jnp.sum(kept, axis=1, keepdims=True))
    scaled = regular * scale_row * scale_column
    error = one - scaled

    def factor(guess, now, product):
        both = product(jnp.concatenate([guess, now], 0), now)
        return guess + both[:size], both[size:]

    guess, now = factor(one + error, nearly(error, error), nearly)
    guess, now = factor(guess, now, nearly)
    total[...] = guess + nearly(guess, now)

    @pl.when(jnp.logical_not(jnp.sum(now * now) < 1e-6))
    def _():
        c = 1.0 / jnp.max(jnp.sum(jnp.abs(scaled), axis=0, keepdims=True))
        smaller = one - c * scaled
        total[...] = c * (one + smaller)
        first = exact(smaller, smaller)
        power[...] = first

        def more(state):
            count, norm = state
            return jnp.logical_and(norm > 1e-6, count < 48)

        def again(state):
            guess, now = factor(total[...], power[...], exact)
            total[...] = guess
            power[...] = now
            return state[0] + 1, jnp.sum(now * now)

        lax.while_loop(more, again, (jnp.int32(0), jnp.sum(first * first)))
        guess = total[...]
        total[...] = guess + exact(guess, one - exact(scaled, guess))

    return total[...] * scale_row * scale_column


def finish_kernel(
    scalars, kept, mine, theirs, upper, lower, rhs, *refs
):
    own, (solution, residual, direction) = refs[:PIECES], refs[PIECES : PIECES + 3]
    stack, total, power, results, done = refs[PIECES + 3 :]
    height, b = rhs.shape
    rows = results.shape[1] // COPIES
    half = mine.shape[0]
    core = scalars[CORE]
    stack[pl.ds(pl.multiple_of(core * half, 8), half), :] = mine[...]
    stack[pl.ds(pl.multiple_of((1 - core) * half, 8), half), :] = theirs[...]
    keep = kept[...].astype(f32)
    row = lax.broadcasted_iota(jnp.int32, (b, b), 0)
    column = lax.broadcasted_iota(jnp.int32, (b, b), 1)
    eye = row == column
    shared = stack[0:b, :]
    turned = shared.T
    regular = jnp.where(row >= column, shared, turned)
    regular = regular + jnp.where(eye, jnp.broadcast_to(1.0 - keep, (b, b)), 0.0)
    diagonal = jnp.broadcast_to(stack[3 * b : 3 * b + 1, :], (b, b))
    squares = jnp.where(row < column, shared, jnp.where(eye, diagonal, turned))
    inverse = inverse_of(regular, eye, total, power)
    weights = exact(inverse, stack[b : 2 * b, :])
    coupled = stack[2 * b : 3 * b, :] - exact(squares, weights)
    correction = exact(inverse, coupled)
    weight_parts = jnp.concatenate(two_parts(weights), 1)
    correction_parts = jnp.concatenate(two_parts(correction), 1)
    packed = joined(own, height)
    copies = []

    def send(which, target, piece):
        part = slice(piece * rows, (piece + 1) * rows)
        copy = pltpu.make_async_copy(results.at[which, part], target.at[part], done.at[which, piece])
        copy.start()
        copies.append(copy)

    for piece in range(COPIES):
        part = slice(piece * rows, (piece + 1) * rows)
        product = dot(packed[part], weight_parts)
        results[0, part, :] = product[:, :b] + product[:, b:]
        send(0, solution, piece)
        moved = dot(upper[part, :], weight_parts)
        moved = moved[:, :b] + moved[:, b:] + dot(lower[part, :], weight_parts[:, :b])
        live = live_rows(scalars, piece * rows, rows, b)
        results[1, part, :] = jnp.where(live, rhs[part, :], 0.0) - moved
        send(1, residual, piece)
    for piece in range(COPIES):
        part = slice(piece * rows, (piece + 1) * rows)
        product = dot(packed[part], correction_parts)
        results[2, part, :] = results[1, part, :] - (product[:, :b] + product[:, b:])
        send(2, direction, piece)
    for copy in copies:
        copy.wait()


def factors(number):
    found, p = [], 2
    while number > 1:
        while number % p == 0:
            found.append(p)
            number //= p
        p += 1
    return found


def rounds_of(clusters, places):
    digits, stride = [], 2
    for radix in factors(places // 2) + factors(clusters):
        digits.append((stride, radix))
        stride *= radix
    groups = []
    for digit in digits:
        if groups and len(groups[-1]) == 1 and groups[-1][0][1] * digit[1] <= 4:
            groups[-1].append(digit)
        else:
            groups.append([digit])

    def moves(group):
        offsets = itertools.product(*[range(radix) for _, radix in reversed(group)])
        return [list(zip(reversed(group), o)) for o in offsets if any(o)][::-1]

    def moved(index, move):
        for (stride, radix), offset in move:
            digit = index // stride % radix
            index += ((digit + offset) % radix - digit) * stride
        return index

    forward = [moves(g) for g in groups]
    backward = forward[::-1]
    if [len(m) for m in forward] != [len(m) for m in backward]:
        backward = forward
    count = clusters * places
    return [
        [
            [(i, moved(i, (first, second)[i % 2])) for i in range(count)]
            for first, second in zip(ours, others)
        ]
        for ours, others in zip(forward, backward)
    ]


def per_device(clusters, places, operator, rhs, interface_sizes, neighbour_rows, kept_columns):
    matrix, right_side = operator[0], rhs[0]
    height, breadth = right_side.shape
    place = lax.axis_index("clu")
    core = lax.axis_index("sub") % 2
    scalars = jnp.stack(
        [interface_sizes[0], place, jnp.int32(clusters - 1), core]
    ).astype(jnp.int32)
    pairing = neighbour_rows.reshape(height // breadth, breadth)
    extra = 2 * pairing.shape[0]
    like = jax.ShapeDtypeStruct
    cost = pl.CostEstimate(
        flops=2 * height * height * breadth, bytes_accessed=2 * height * height, transcendentals=0
    )
    piece = height // PIECES
    shapes = [like((piece, breadth), bf16)] * (PIECES - 1) + [like((piece + extra, breadth), bf16)]
    *packed, listed = pl.pallas_call(
        round_kernel,
        out_shape=(*shapes, like(pairing.shape, f32)),
        in_specs=[SMEM] + [HBM] * 3,
        out_specs=(VMEM,) * (PIECES + 1),
        scratch_shapes=[
            pltpu.VMEM((height, breadth), f32),
            pltpu.VMEM((1, breadth), jnp.int32),
            pltpu.VMEM(pairing.shape, jnp.int32),
            pltpu.SemaphoreType.DMA((3,)),
        ],
        compiler_params=parameters(),
        name="round",
    )(interface_sizes, *map(in_hbm, (right_side, kept_columns, pairing)))
    pairs = [(i, i ^ 1) for i in range(clusters)]
    other = [lax.ppermute(part, "clu", pairs) for part in packed]
    strips = height // min(height, 256)
    base = pl.pallas_call(
        local_kernel,
        out_shape=like((height, breadth), f32),
        in_specs=[SMEM, HBM] + [VMEM] * PIECES,
        out_specs=VMEM,
        scratch_shapes=[pltpu.VMEM((height, height), bf16), pltpu.SemaphoreType.DMA((strips,))],
        compiler_params=parameters(),
        cost_estimate=cost,
        name="local",
    )(scalars, in_hbm(matrix), *packed)
    other[0], base = lax.optimization_barrier((other[0], base))
    onward = [(i, i + 2 if i + 2 < clusters else i + 1) for i in range(0, clusters, 2)]
    onward += [(i, max(i - 2, 0)) for i in range(1, clusters, 2)]
    outside = [lax.ppermute(part, "clu", onward) for part in other]
    nearer, turned, parts, projected = pl.pallas_call(
        near_kernel,
        out_shape=(
            like((height, breadth), f32),
            like((breadth, height), bf16),
            like((height, 2 * breadth), bf16),
            like((breadth, breadth), f32),
        ),
        in_specs=[SMEM] + [VMEM] * (3 + 2 * PIECES),
        out_specs=(VMEM,) * 4,
        compiler_params=parameters(),
        cost_estimate=cost,
        name="near",
    )(scalars, listed, base, right_side, *other, *packed)
    half = (3 * breadth + 16) // 2
    upper, lower, mine, theirs = pl.pallas_call(
        sums_kernel,
        out_shape=(
            like((height, breadth), bf16),
            like((height, breadth), bf16),
            like((half, breadth), f32),
            like((half, breadth), f32),
        ),
        in_specs=[SMEM] + [VMEM] * (5 + PIECES),
        out_specs=(VMEM,) * 4,
        scratch_shapes=[
            pltpu.VMEM((height, breadth), f32),
            pltpu.VMEM((2 * half, breadth), f32),
        ],
        compiler_params=parameters(),
        name="sums",
    )(scalars, listed, nearer, turned, parts, projected, *outside)
    swap = [(i, i ^ 1) for i in range(clusters * places)]
    mine = mine + lax.ppermute(theirs, AXES, swap)
    for routes in rounds_of(clusters, places):
        parts = [mine] + [lax.ppermute(mine, AXES, route) for route in routes]
        while len(parts) > 1:
            parts = [sum(parts[i : i + 2][1:], parts[i]) for i in range(0, len(parts), 2)]
        mine = parts[0]
    theirs = lax.ppermute(mine, AXES, swap)
    outs = pl.pallas_call(
        finish_kernel,
        out_shape=(like((height, breadth), f32),) * 3,
        in_specs=[SMEM] + [VMEM] * (6 + PIECES),
        out_specs=(HBM,) * 3,
        scratch_shapes=[
            pltpu.VMEM((2 * half, breadth), f32),
            pltpu.VMEM((breadth, breadth), f32),
            pltpu.VMEM((breadth, breadth), f32),
            pltpu.VMEM((3, height, breadth), f32),
            pltpu.SemaphoreType.DMA((3, COPIES)),
        ],
        compiler_params=parameters(),
        name="finish",
    )(scalars, kept_columns, mine, theirs, upper, lower, right_side, *packed)
    return tuple(out[None] for out in outs)


def solution(mesh):
    clusters, places = mesh.shape["clu"], mesh.shape["sub"]
    return jax.shard_map(
        functools.partial(per_device, clusters, places),
        mesh=mesh,
        in_specs=(
            P(("clu", "sub"), None, None),
            P(("clu", "sub"), None, None),
            P(("clu", "sub")),
            P(("clu", "sub"), None),
            P(),
        ),
        out_specs=(P(("clu", "sub"), None, None),) * 3,
        check_vma=False,
    )
```
